512 devices in a mesh: ex: 64 (over z_hi, y, x), feat: 8 (over z_lo, core).
Axes of the slice: x: 4, y: 4, z: 16 (z_hi: 4, z_lo: 4; z = z_hi * 4 + z_lo), core: 2. Of those that a mesh axis runs over, the one named last changes fastest.
Arguments:
- grads: bfloat16 [8192, 8192], P('ex', 'feat')
Outputs:
- tiles: float32 [64, 1024, 1024], P('ex', 'feat')
All inputs are finite; a program needn't handle non-finite values.
Results may differ from the reference program's by a relative error of at most 0.0041.
Values may be sent and summed in bfloat16 or wider, within the bound.
A program may use at most 64 MiB of HBM per device.

```python
import math
import jax
import jax.numpy as jnp
from jax import lax

FEATS = 8192
ROWS_DEV = 128
EXAMPLES = 8192
ROWGROUP = 8
COLGROUP = 8
N_EX = 64


def draw_grads(key, part):
    key = jax.random.fold_in(key, 11)
    first, second, third = jax.random.split(key, 3)
    noise = jax.random.normal(first, (EXAMPLES, FEATS), jnp.float32)
    rowscale = jnp.exp(jax.random.uniform(second, (EXAMPLES, 1), jnp.float32, 0.0, math.log(10.0)))
    ramp = jnp.exp(math.log(3.0) * jnp.arange(FEATS, dtype=jnp.float32) / FEATS)
    colscale = jnp.exp(jax.random.uniform(third, (1, FEATS), jnp.float32, 0.0, math.log(10.0))) * ramp[None, :]
    return (noise * rowscale * colscale * 0.1).astype(jnp.bfloat16)


def setup_inputs(seed: int = 0) -> dict:
    streams_of = jax.random.split(jax.random.key(seed), 2)
    return {
        "grads": draw_grads(jax.random.fold_in(streams_of[1], 71), 0),
    }


def reference(grads):
    wide = grads.astype(jnp.float32)
    sumsq = lax.optimization_barrier(jnp.sum(wide * wide, axis=1, keepdims=True))
    unit = (wide / jnp.sqrt(sumsq + 1e-06)).astype(jnp.bfloat16)
    score = jnp.dot(unit, unit.T, preferred_element_type=jnp.float32) * math.sqrt(FEATS)
    ids = jnp.arange(EXAMPLES, dtype=jnp.int32)
    score = jnp.where(ids[:, None] == ids[None, :], jnp.float32(0.0), score)
    blocks = score.reshape(COLGROUP, ROWGROUP * ROWS_DEV, COLGROUP, ROWGROUP, ROWS_DEV)
    blocks = jnp.transpose(blocks, (0, 3, 1, 2, 4))
    return blocks.reshape(N_EX, ROWGROUP * ROWS_DEV, COLGROUP * ROWS_DEV)
```

```python
import functools
import math

import jax
import jax.numpy as jnp
from jax import lax
from jax.experimental import pallas as pl
from jax.experimental.pallas import tpu as pltpu
from jax.sharding import PartitionSpec as P

MESH = pl.DeviceIdType.MESH
NZ = 16
ROWS = 128
WIDTH = 1024
CHUNKS = 4
PIECE = ROWS // CHUNKS
RING = CHUNKS * 15 // 2
RUN_RING = True
RUN_XY = True
RUN_MATH = True


def kernel(
    g_ref, out_ref, cols, rows, acc, colsq, rowsq, sqsend, sqrecv, half, swap_out, swap_in,
    load_sem, ring_send, ring_recv, xy_send, xy_recv, tail_send, tail_recv,
):
    ex = lax.axis_index("ex")
    feat = lax.axis_index("feat")
    h, y, x = ex // 16, ex // 4 % 4, ex % 4
    l, c = feat // 2, feat % 2
    z = h * 4 + l
    big_y = y // 2
    dx = (x - l % 2 * 2 + 4) % 4
    dy = (y - l // 2 + 4) % 4

    def device(zz, yy, xx, cc):
        return (zz // 4 * 16 + yy * 4 + xx, zz % 4 * 2 + cc)

    zu, zd = device((z + 1) % NZ, y, x, c), device((z + NZ - 1) % NZ, y, x, c)
    xu, xd = device(z, y, (x + 1) % 4, c), device(z, y, (x + 3) % 4, c)
    yu, yd = device(z, (y + 1) % 4, x, c), device(z, (y + 3) % 4, x, c)
    opposite = device(z, (y + 2) % 4, x, c)
    sibling = device(z, y, x, 1 - c)

    load = pltpu.make_async_copy(g_ref, cols.at[z], load_sem.at[0])
    load.start()
    barrier = pltpu.get_barrier_semaphore()
    for to in (zu, zd, xu, xd, yu, yd, opposite, sibling):
        pl.semaphore_signal(barrier, inc=1, device_id=to, device_id_type=MESH)
    pl.semaphore_wait(barrier, 8)
    load.wait()

    sent = []

    def remote(src, dst, send, recv, to):
        return pltpu.make_async_remote_copy(
            src_ref=src, dst_ref=dst, send_sem=send, recv_sem=recv, device_id=to,
            device_id_type=MESH,
        )

    def ring_copy(way, n):
        far, j = n // CHUNKS, n % CHUNKS
        if way == 1:
            j = CHUNKS - 1 - j
        owner = (z - far + NZ) % NZ if way == 0 else (z + far) % NZ
        ref = cols.at[owner, pl.ds(j * PIECE, PIECE)]
        return remote(ref, ref, ring_send.at[way, n], ring_recv.at[way, n], zu if way == 0 else zd)

    def ring_arrival(way, n):
        far, j = n // CHUNKS + 1, n % CHUNKS
        if way == 1:
            j = CHUNKS - 1 - j
        owner = (z - far + NZ) % NZ if way == 0 else (z + far) % NZ
        ref = cols.at[owner, pl.ds(j * PIECE, PIECE)]
        return remote(ref, ref, ring_send.at[way, n], ring_recv.at[way, n], zu if way == 0 else zd)

    def ring_start(n):
        for way in range(2):
            ring_copy(way, n).start()

    def ring_round(n):
        for way in range(2):
            ring_arrival(way, n).wait_recv()
            if n + CHUNKS < RING:
                ring_copy(way, n + CHUNKS).start()

    low, high = pl.ds(0, 64), pl.ds(64, 64)
    source = (dx < 2) & (dy % 2 == 0)
    own_y = dy // 2

    def slice_of(k):
        return (l, l + 1 - l % 2 * 2, (l + 2) % 4, 3 - l)[k]

    def a_at(k, yy, i):
        return rows.at[slice_of(k), 2 * yy + i]

    def a_pair(k, yy):
        return rows.at[slice_of(k), pl.ds(2 * yy, 2)]

    def b_at(k, yy, i):
        return rows.at[slice_of(k), 4 + 2 * i + yy]

    def b_pair(k, i):
        return rows.at[slice_of(k), pl.ds(4 + 2 * i, 2)]

    def go(k, sem, recv, src, dst, to, cond):
        remote(src, dst, xy_send.at[k, sem], xy_recv.at[k, recv], to).start()
        sent.append((cond, k, sem, len(src.shape) == 3))

    def await_(k, recv, dst):
        remote(dst, dst, xy_send.at[k, 0], xy_recv.at[k, recv], xu).wait_recv()

    even, left = dy % 2 == 0, dx < 2
    odd, right = dy % 2 == 1, dx >= 2
    even_left, even_right, odd_left = even & left, even & right, odd & left
    even_2, even_3 = even & (dx == 2), even & (dx == 3)
    dx_2, dx_3, dy_1, dy_3 = dx == 2, dx == 3, dy == 1, dy == 3

    def step1(k):
        @pl.when(source)
        def _():
            shard = h * 4 + slice_of(k)
            first = pltpu.make_async_copy(
                cols.at[shard, low], a_at(k, own_y, dx), load_sem.at[1])
            second = pltpu.make_async_copy(
                cols.at[shard, high], b_at(k, own_y, dx), load_sem.at[2])
            first.start()
            second.start()
            go(k, 0, 0, cols.at[shard, low], a_at(k, own_y, dx), xu, source)
            go(k, 2, 2 + own_y, cols.at[shard, high], b_at(k, own_y, dx), yu, source)
            go(k, 1, 0, cols.at[shard, low], a_at(k, own_y, dx), xd, source)
            go(k, 3, 2 + own_y, cols.at[shard, high], b_at(k, own_y, dx), yd, source)
            first.wait()
            second.wait()

    def a3(k, cond):
        go(k, 6, 5 + own_y, a_pair(k, own_y), a_pair(k, own_y), yu, cond)
        go(k, 7, 5 + own_y, a_pair(k, own_y), a_pair(k, own_y), yd, cond)

    def b3(k, cond):
        go(k, 10, 9, b_pair(k, dx), b_pair(k, dx), xu, cond)
        go(k, 11, 9, b_pair(k, dx), b_pair(k, dx), xd, cond)

    def step2(k):
        @pl.when(even)
        def _():
            await_(k, 0, a_at(k, own_y, (dx + 1) % 2))

            @pl.when(dx_2)
            def _():
                go(k, 4, 1, a_at(k, own_y, 1), a_at(k, own_y, 1), xu, even_2)

            @pl.when(dx_3)
            def _():
                go(k, 4, 1, a_at(k, own_y, 0), a_at(k, own_y, 0), xd, even_3)

            @pl.when(left)
            def _():
                a3(k, even_left)

        @pl.when(odd_left)
        def _():
            await_(k, 2, b_at(k, 0, dx))
            await_(k, 3, b_at(k, 1, dx))
            go(k, 5, 4, b_at(k, own_y, dx), b_at(k, own_y, dx), yu, odd_left)
            b3(k, odd_left)

    def step3(k):
        @pl.when(even_right)
        def _():
            await_(k, 1, a_at(k, own_y, dx % 2))
            a3(k, even_right)

        @pl.when(even_left)
        def _():
            await_(k, 4, b_at(k, 1 - own_y, dx))
            b3(k, even_left)

    def step4(k):
        @pl.when(odd)
        def _():
            await_(k, 5, a_pair(k, 0))
            await_(k, 6, a_pair(k, 1))

            @pl.when(dy_1)
            def _():
                go(k, 8, 7, a_at(k, 0, 0), a_at(k, 0, 0), yu, dy_1)
                go(k, 9, 7, a_at(k, 1, 0), a_at(k, 1, 0), yd, dy_1)

            @pl.when(dy_3)
            def _():
                go(k, 8, 8, a_at(k, 0, 1), a_at(k, 0, 1), yd, dy_3)
                go(k, 9, 8, a_at(k, 1, 1), a_at(k, 1, 1), yu, dy_3)

        await_(k, 9, b_pair(k, (dx + 1) % 2))

        @pl.when(dx_2)
        def _():
            go(k, 12, 10, b_pair(k, 1), b_pair(k, 1), xu, dx_2)

        @pl.when(dx_3)
        def _():
            go(k, 12, 10, b_pair(k, 0), b_pair(k, 0), xd, dx_3)

    def step5(k):
        @pl.when(even)
        def _():
            await_(k, 7, a_at(k, 1 - own_y, 0))
            await_(k, 8, a_at(k, 1 - own_y, 1))

        @pl.when(right)
        def _():
            await_(k, 10, b_pair(k, dx % 2))

    def squares(block):
        wide = block.astype(jnp.float32)
        wide = wide * wide
        total = wide[:, :128]
        for piece in range(1, WIDTH // 128):
            total = total + wide[:, piece * 128:piece * 128 + 128]
        return total

    def multiply(shard):
        hh, ll = shard // 4, shard % 4
        block = cols[shard]
        acc[hh] += lax.dot_general(
            rows[ll].reshape(512, WIDTH), block, (((1,), (1,)), ((), ())),
            preferred_element_type=jnp.float32,
        )
        colsq[hh] += squares(block)

    def row_squares():
        for ll in range(4):
            for part in range(8):
                rowsq[part] += squares(rows[ll, part])

    if RUN_MATH:
        acc[...] = jnp.zeros_like(acc)
        colsq[...] = jnp.zeros_like(colsq)
        rowsq[...] = jnp.zeros_like(rowsq)

    plan = {}
    if RUN_XY:
        for k in range(4):
            plan.setdefault(2 * k, []).append((step1, k))
            plan.setdefault(3 * k + 1, []).append((step2, k))
            plan.setdefault(3 * k + 2, []).append((step3, k))
            plan.setdefault(3 * k + 4, []).append((step4, k))
            plan.setdefault(99, []).append((step5, k))

    if RUN_RING:
        for n in range(CHUNKS):
            ring_start(n)
    unit = CHUNKS // 2
    for tick in range(16):
        for step, k in plan.get(tick, ()):
            step(k)
        if RUN_RING and tick < 15:
            for n in range(tick * unit, (tick + 1) * unit):
                ring_round(n)
    for step, k in plan.get(99, ()):
        step(k)

    if RUN_MATH:
        row_squares()

        def body(s, carry):
            multiply(s)
            return carry

        lax.fori_loop(0, NZ, body, 0)

        eye = lax.broadcasted_iota(jnp.int32, (128, 128), 0) == lax.broadcasted_iota(
            jnp.int32, (128, 128), 1)

        def to_lanes(column):
            return jnp.sum(jnp.where(eye, column, 0.0), axis=0, keepdims=True)

        def to_rows(lanes):
            return jnp.sum(jnp.where(eye, lanes, 0.0), axis=1, keepdims=True)

        for hh in range(4):
            sqsend[hh:hh + 1] = to_lanes(jnp.sum(colsq[hh], axis=1, keepdims=True))
        for yy in range(2):
            for i in range(2):
                both = jnp.concatenate([rowsq[2 * yy + i], rowsq[4 + 2 * i + yy]], axis=0)
                sqsend[4 + 2 * yy + i:5 + 2 * yy + i] = to_lanes(
                    jnp.sum(both, axis=1, keepdims=True))
        squares_swap = remote(sqsend, sqrecv, tail_send.at[0], tail_recv.at[0], sibling)
        squares_swap.start()

        other = 1 - c
        for yy in range(2):
            for hh in range(4):
                swap_out[yy, hh, :64] = acc[hh, pl.ds(pl.multiple_of((2 * yy + other) * 64, 64), 64)]
                swap_out[yy, hh, 64:] = acc[
                    hh, pl.ds(pl.multiple_of((4 + 2 * other + yy) * 64, 64), 64)]
        halves = remote(swap_out, swap_in, tail_send.at[1], tail_recv.at[1], sibling)
        halves.start()
        squares_swap.wait()
        inverse = lax.rsqrt(sqsend[...] + sqrecv[...] + 1e-6)
        halves.wait()

        def result(yy, hh):
            row_scale = to_rows(
                jnp.where(c == 0, inverse[4 + 2 * yy:5 + 2 * yy], inverse[5 + 2 * yy:6 + 2 * yy]))
            col_scale = inverse[hh:hh + 1]
            top = acc[hh, pl.ds(pl.multiple_of((2 * yy + c) * 64, 64), 64)]
            bottom = acc[hh, pl.ds(pl.multiple_of((4 + 2 * c + yy) * 64, 64), 64)]
            raw = jnp.concatenate([top, bottom], axis=0) + swap_in[yy, hh]
            value = raw * row_scale * (col_scale * math.sqrt(8192.0))
            value = jnp.where((row_scale > 0.0) & (col_scale > 0.0), value, 0.0)
            same = (hh == h) & (yy == big_y) & (2 * l + c == ex % 8)
            return jnp.where(eye & same, 0.0, value)

        for hh in range(4):
            for yy in range(2):
                @pl.when(yy != big_y)
                def _():
                    half[0, hh] = result(yy, hh).astype(jnp.bfloat16)
        across = remote(half.at[0], half.at[1], tail_send.at[2], tail_recv.at[2], opposite)
        across.start()
        for hh in range(4):
            for yy in range(2):
                @pl.when(yy == big_y)
                def _():
                    out_ref[0, :, (2 * hh + yy) * 128:(2 * hh + yy + 1) * 128] = result(yy, hh)
        across.wait()
        for hh in range(4):
            for yy in range(2):
                @pl.when(yy != big_y)
                def _():
                    out_ref[0, :, (2 * hh + yy) * 128:(2 * hh + yy + 1) * 128] = half[1, hh].astype(
                        jnp.float32)
    else:
        out_ref[...] = jnp.zeros_like(out_ref)

    if RUN_RING:
        for n in range(RING):
            for way in range(2):
                ring_copy(way, n).wait_send()
    for cond, k, sem, pair in sent:
        @pl.when(cond)
        def _():
            ref = rows.at[0, pl.ds(0, 2)] if pair else rows.at[0, 0]
            remote(ref, ref, xy_send.at[k, sem], xy_recv.at[k, 0], xu).wait_send()


def local(grads):
    return pl.pallas_call(
        kernel,
        out_shape=jax.ShapeDtypeStruct((1, 128, 1024), jnp.float32),
        in_specs=[pl.BlockSpec(memory_space=pl.ANY)],
        out_specs=pl.BlockSpec(memory_space=pltpu.VMEM),
        scratch_shapes=[
            pltpu.VMEM((NZ, ROWS, WIDTH), jnp.bfloat16),
            pltpu.VMEM((4, 8, 64, WIDTH), jnp.bfloat16),
            pltpu.VMEM((4, 512, 128), jnp.float32),
            pltpu.VMEM((4, 128, 128), jnp.float32),
            pltpu.VMEM((8, 64, 128), jnp.float32),
            pltpu.VMEM((8, 128), jnp.float32),
            pltpu.VMEM((8, 128), jnp.float32),
            pltpu.VMEM((2, 4, 128, 128), jnp.bfloat16),
            pltpu.VMEM((2, 4, 128, 128), jnp.float32),
            pltpu.VMEM((2, 4, 128, 128), jnp.float32),
            pltpu.SemaphoreType.DMA((3,)),
            pltpu.SemaphoreType.DMA((2, RING)),
            pltpu.SemaphoreType.DMA((2, RING)),
            pltpu.SemaphoreType.DMA((4, 13)),
            pltpu.SemaphoreType.DMA((4, 11)),
            pltpu.SemaphoreType.DMA((3,)),
            pltpu.SemaphoreType.DMA((3,)),
        ],
        compiler_params=pltpu.CompilerParams(
            collective_id=0, has_side_effects=True, vmem_limit_bytes=32 * 1024 * 1024
        ),
        cost_estimate=pl.CostEstimate(
            flops=2 * 512 * 512 * 4096, bytes_accessed=1 << 20, transcendentals=0),
    )(grads)


def solution(mesh):
    return jax.shard_map(
        local,
        mesh=mesh,
        in_specs=(P("ex", "feat"),),
        out_specs=P("ex", "feat", None),
        check_vma=False,
    )
```

```python
import math

import jax
import jax.numpy as jnp
from jax import lax
from jax.experimental import pallas as pl
from jax.experimental.pallas import tpu as pltpu
from jax.sharding import PartitionSpec as P

MESH = pl.DeviceIdType.MESH
NZ = 16
ROWS = 128
WIDTH = 1024
CHUNKS = 4
PIECE = 32
RING = 30
RUN_RING = True
RUN_XY = True
RUN_MATH = True
P_TICKS = (16, 20, 21, 24, 25)
SQ_TICKS = (13, 17, 22, 26)
EVENTS = (
    (51561376, 76382242, 52086690, 75858976, 42126276, 85805126, 42651590, 85281860, 67453349, 68995716, 67978663,
     68472454, 68520385, 67945088, 69045699, 67421826),
    (1495976, 11046020, 2021290, 10520710, 449484, 20464768, 974798, 19939458, 1575341, 17056896, 1052079,
     67387522, 524745, 9735300, 1483, 68454534),
    (890882, 397000, 367616, 920266, 1921030, 1443500, 1397764, 1966766, 69554183, 36756227, 70079493, 37281347,
     70621187, 35705607, 71146497, 36230695),
    (96952326, 20519211, 97477636, 37263657, 98019330, 11080015, 98544640, 36196685, 114558466, 35654927,
     115081728, 36178189, 121900550, 36701451, 122423812, 37224713),
    (2625037, 71066629, 2099727, 70541319, 3671561, 70036481, 3146251, 69511171, 3939340, 70029866, 3414030,
     19796520, 2888712, 71064142, 2363402, 12458572),
    (115349204, 80483024, 115872470, 79959762, 124788400, 89922228, 125311666, 89398966, 2761392, 73214069,
     2238130, 72690807, 3812052, 72163441, 3288790, 71640179),
    (5512569, 15248532, 6035835, 14756948, 4461949, 24667280, 4985215, 24192048, 5470731, 13180942, 5996041,
     12657676, 4436495, 22620170, 4961805, 22096904),
    (57680911, 56765965, 58204173, 57289231, 48245771, 49423881, 48769033, 49947147, 48246294, 32908881, 48769556,
     33335057, 57681426, 31862325, 58204688, 32272149),
    (7613459, 40903483, 8136721, 24127289, 6562839, 39856991, 7086101, 14692189, 4990233, 5914268, 4464923,
     5388958, 6040861, 4863640, 5515551, 4338330),
    (7091223, 5652062, 6565909, 6175390, 8141843, 4601402, 7616529, 5124762, 8141852, 23360664, 7616542, 73691290,
     7091224, 16039068, 6565914, 74758302),
    (15902, 14873, 14876, 15899, 13850, 12829, 12824, 13855, 13850, 15643, 12824, 14427, 15902, 13599, 14876, 12351),
)
DONE = (
    (101462146, 50864128, 101462146, 50864128, 101462146, 50864128, 101462146, 50864128, 17043456, 0, 17043456, 0,
     17043456, 0, 17043456, 0),
    (238068167, 203718981, 238068167, 203718981, 238068167, 203718981, 238068167, 203718981, 136069315, 152846531,
     136069315, 152846531, 136069315, 152846531, 136069315, 152846531),
    (391464015, 340857869, 391464015, 340857869, 391464015, 340857869, 391464015, 340857869, 289469195, 305984203,
     289469195, 305984203, 289469195, 305984203, 289469195, 305984203),
    (494253720, 510772760, 494253720, 510772760, 494253720, 510772760, 494253720, 510772760, 459638100, 459634003,
     459638100, 459634003, 459638100, 459634003, 459638100, 459634003),
    (545392607, 545388510, 545392607, 545388510, 545392607, 545388510, 545392607, 545388510, 545384348, 545388509,
     545384348, 545388509, 545384348, 545388509, 545384348, 545388509),
    (133152, 133152, 133152, 133152, 133152, 133152, 133152, 133152, 133152, 133152, 133152, 133152, 133152,
     133152, 133152, 133152),
)


def kernel(
    g_ref, out_ref, cols, rows, acc, colsq, rowsq, sq_out, sq_in, swap_in, half_out, half_in,
    load_sem, ring_send, ring_recv, xy_send, xy_recv, tail_send, tail_recv,
):
    ex = lax.axis_index("ex")
    feat = lax.axis_index("feat")
    h, y, x = ex // 16, ex // 4 % 4, ex % 4
    l, c = feat // 2, feat % 2
    z = h * 4 + l
    big_y = y // 2
    dx = (x - l % 2 * 2 + 4) % 4
    dy = (y - l // 2 + 4) % 4

    def device(zz, yy, xx, cc):
        return (zz // 4 * 16 + yy * 4 + xx, zz % 4 * 2 + cc)

    z_up, z_down = device((z + 1) % NZ, y, x, c), device((z + NZ - 1) % NZ, y, x, c)
    plane = (
        device(z, y, (x + 1) % 4, c), device(z, y, (x + 3) % 4, c),
        device(z, (y + 1) % 4, x, c), device(z, (y + 3) % 4, x, c),
    )
    opposite = device(z, (y + 2) % 4, x, c)
    sibling = device(z, y, x, 1 - c)

    def remote(src, dst, send, recv, to):
        return pltpu.make_async_remote_copy(
            src_ref=src, dst_ref=dst, send_sem=send, recv_sem=recv, device_id=to,
            device_id_type=MESH,
        )

    load = pltpu.make_async_copy(g_ref, cols.at[z], load_sem)
    load.start()
    barrier = pltpu.get_barrier_semaphore()
    for to in (z_up, z_down, *plane, opposite, sibling):
        pl.semaphore_signal(barrier, inc=1, device_id=to, device_id_type=MESH)
    acc[...] = jnp.zeros_like(acc)
    colsq[...] = jnp.zeros_like(colsq)
    load.wait()
    pl.semaphore_wait(barrier, 8)

    def ring_copy(way, n, far):
        j = n % CHUNKS if way == 0 else CHUNKS - 1 - n % CHUNKS
        owner = (z - far + NZ) % NZ if way == 0 else (z + far) % NZ
        ref = cols.at[owner, j]
        to = z_up if way == 0 else z_down
        return remote(ref, ref, ring_send.at[way, n], ring_recv.at[way, n], to)

    def ring_start(n):
        for way in range(2):
            ring_copy(way, n, n // CHUNKS).start()

    def ring_round(n):
        for way in range(2):
            ring_copy(way, n, n // CHUNKS + 1).wait_recv()
            if n + CHUNKS < RING:
                ring_copy(way, n + CHUNKS, n // CHUNKS + 1).start()

    def ring_sent(n):
        for way in range(2):
            ring_copy(way, n, 0).wait_send()

    place = dx * 4 + dy
    source = (dx < 2) & (dy % 2 == 0)

    def here(table):
        value = jnp.int32(table[0])
        for index, entry in enumerate(table[1:], 1):
            value = jnp.where(place == index, jnp.int32(entry), value)
        return value

    events = [here(table) for table in EVENTS]
    done = [here(table) for table in DONE]
    handled = [jnp.int32(0)] + [done[n // 5] // 64 ** (n % 5) % 64 for n in range(28)]

    def slice_of(k):
        return (l // 2 + k // 2) % 2 * 2 + (l + k) % 2

    def own_copy(k, part):
        q = 2 * (2 * dx + dy // 2) + part
        return pltpu.make_async_copy(
            cols.at[h * 4 + slice_of(k), pl.ds(2 * part, 2)],
            rows.at[slice_of(k), pl.ds(2 * q, 2)], xy_recv.at[k, q],
        )

    def set_out(k):
        @pl.when(source)
        def _():
            for part in range(2):
                own_copy(k, part).start()

    def decoded(e):
        third = e // 3
        word = events[0]
        for index in range(1, len(events)):
            word = jnp.where(third == index, events[index], word)
        digit = jnp.right_shift(word, (e - third * 3) * 9)
        return digit // 8 % 4, digit % 8, [digit // (32 * 2**d) % 2 == 1 for d in range(4)]

    def onward(k, q, d):
        ref = rows.at[slice_of(k), pl.ds(2 * q, 2)]
        return remote(ref, ref, xy_send.at[k, 4 * q + d], xy_recv.at[k, q], plane[d])

    def take(e, carry):
        k, q, goes = decoded(e)
        onward(k, q, 0).wait_recv()
        for d in range(4):
            pl.when(goes[d])(onward(k, q, d).start)
        return carry

    def take_until(n):
        lax.fori_loop(handled[n], handled[n + 1], take, 0)

    def xy_sent():
        def body(e, carry):
            k, q, goes = decoded(e)
            for d in range(4):
                pl.when(goes[d])(onward(k, q, d).wait_send)
            return carry

        lax.fori_loop(0, 32, body, 0)

    def squares(block):
        wide = block.astype(jnp.float32)
        wide = wide * wide
        total = wide[:, :128]
        for part in range(1, WIDTH // 128):
            total = total + wide[:, part * 128:part * 128 + 128]
        return total

    def cube(b):
        return (h + b + b // 2 - b // 3 * 2) % 4

    def multiply(b, k):
        ll = slice_of(k)
        block = cols[cube(b) * 4 + ll].reshape(ROWS, WIDTH)
        product = lax.dot_general(
            rows[ll].reshape(4 * ROWS, WIDTH), block, (((1,), (1,)), ((), ())),
            preferred_element_type=jnp.float32,
        )
        acc[b] += product.reshape(4, ROWS, 128)
        colsq[b] += squares(block)

    def multiply_all(k, blocks):
        def body(i, carry):
            b = blocks[0]
            for index in range(1, len(blocks)):
                b = jnp.where(i == index, blocks[index], b)
            multiply(b % 4, k)
            return carry

        lax.fori_loop(0, len(blocks), body, 0)

    def row_squares(k):
        ll = slice_of(k)

        def body(i, carry):
            total = squares(rows[ll, pl.ds(4 * i, 4)].reshape(ROWS, WIDTH))
            if k:
                total = total + rowsq[i]
            rowsq[i] = total
            return carry

        lax.fori_loop(0, 4, body, 0)

    eye = lax.broadcasted_iota(jnp.int32, (128, 128), 0) == lax.broadcasted_iota(
        jnp.int32, (128, 128), 1)

    def to_lanes(folded):
        column = jnp.sum(folded, axis=1, keepdims=True)
        return jnp.sum(jnp.where(eye, column, 0.0), axis=0, keepdims=True)

    def to_rows(lanes):
        return jnp.sum(jnp.where(eye, lanes, 0.0), axis=1, keepdims=True)

    last = jnp.where(l == 0, 1, jnp.where(l == 3, 2, 3))

    far = jnp.where(l < 2, 1, 2)
    plan = {
        P_TICKS[0]: lambda: multiply_all(0, (0, 1, 2)),
        P_TICKS[1]: lambda: multiply_all(1, (0, 1, 2)),
        P_TICKS[2]: lambda: multiply_all(2, (0, 3 - far)),
        P_TICKS[3]: lambda: multiply_all(2, (far, 3)),
        P_TICKS[4]: lambda: multiply_all(3, (last + 1, last + 2, last + 3)),
    }
    if RUN_RING:
        for n in range(CHUNKS):
            ring_start(n)
    for tick in range(28):
        if RUN_XY:
            if tick % CHUNKS == 0 and tick < 4 * CHUNKS:
                set_out(tick // CHUNKS)
            take_until(tick)
        if RUN_MATH:
            if tick in SQ_TICKS:
                row_squares(SQ_TICKS.index(tick))
            if tick in plan:
                plan[tick]()
        if RUN_RING:
            ring_round(tick)

    other = 1 - c
    if RUN_MATH:
        multiply(3, 1)
        multiply(last, 3)
        for b in range(3):
            sq_out[0, b:b + 1] = to_lanes(colsq[b])
        for p in range(4):
            sq_out[0, 4 + p:5 + p] = to_lanes(rowsq[p])
        swaps = [
            remote(sq_out.at[0], sq_in.at[0], tail_send.at[0], tail_recv.at[0], sibling),
            remote(
                acc.at[pl.ds(0, 3), pl.ds(2 * other, 2)], swap_in.at[pl.ds(0, 3)], tail_send.at[1],
                tail_recv.at[1], sibling),
            remote(sq_out.at[1], sq_in.at[1], tail_send.at[2], tail_recv.at[2], sibling),
            remote(
                acc.at[3, pl.ds(2 * other, 2)], swap_in.at[3], tail_send.at[3], tail_recv.at[3],
                sibling),
        ]
        swaps[0].start()
        swaps[1].start()

    if RUN_XY:
        xy_sent()
    if RUN_RING:
        for n in range(RING - CHUNKS):
            ring_sent(n)
        for n in range(28, RING):
            ring_round(n)

    if RUN_MATH:
        multiply(3, 0)
        sq_out[1] = jnp.broadcast_to(to_lanes(colsq[3]), (8, 128))
        swaps[2].start()
        swaps[3].start()
        swaps[0].wait()
        scales = lax.rsqrt(sq_out[0] + sq_in[0] + 1e-6)
        swaps[1].wait()
        row_scale = [
            to_rows(jnp.where(c == 0, scales[4 + yy:5 + yy], scales[6 + yy:7 + yy]))
            for yy in range(2)
        ]
        row_here = jnp.where(big_y == 0, row_scale[0], row_scale[1])
        row_there = jnp.where(big_y == 0, row_scale[1], row_scale[0])

        def result(b, yy, row_side, col_side):
            raw = acc[b, 2 * c + yy] + swap_in[b, yy]
            value = raw * row_side * (col_side * math.sqrt(8192.0))
            return jnp.where((row_side > 0.0) & (col_side > 0.0), value, 0.0)

        for b in range(3):
            half_out[b] = result(b, 1 - big_y, row_there, scales[b:b + 1]).astype(jnp.bfloat16)
        across = [
            remote(
                half_out.at[pl.ds(0, 3)], half_in.at[pl.ds(0, 3)], tail_send.at[4],
                tail_recv.at[4], opposite),
            remote(half_out.at[3], half_in.at[3], tail_send.at[5], tail_recv.at[5], opposite),
        ]
        across[0].start()
        swaps[2].wait()
        scale = lax.rsqrt(sq_out[1] + sq_in[1] + 1e-6)[:1]
        swaps[3].wait()
        half_out[3] = result(3, 1 - big_y, row_there, scale).astype(jnp.bfloat16)
        across[1].start()

        def store(b, yy, value):
            at = pl.multiple_of((2 * cube(b) + yy) * 128, 128)
            out_ref[0, :, pl.ds(at, 128)] = value

        for b in range(4):
            value = result(b, big_y, row_here, scales[b:b + 1] if b < 3 else scale)
            if b == 0:
                value = jnp.where(eye & (2 * l + c == ex % 8), 0.0, value)
            store(b, big_y, value)
        across[0].wait()
        for b in range(3):
            store(b, 1 - big_y, half_in[b].astype(jnp.float32))
        across[1].wait()
        store(3, 1 - big_y, half_in[3].astype(jnp.float32))
    else:
        out_ref[...] = jnp.zeros_like(out_ref)
    if RUN_RING:
        for n in range(RING - CHUNKS, RING):
            ring_sent(n)


def local(grads):
    dma = pltpu.SemaphoreType.DMA
    out = pl.pallas_call(
        kernel,
        out_shape=jax.ShapeDtypeStruct((1, 128, 1024), jnp.float32),
        in_specs=[pl.BlockSpec(memory_space=pl.ANY)],
        out_specs=pl.BlockSpec(memory_space=pltpu.VMEM),
        scratch_shapes=[
            pltpu.VMEM((NZ, CHUNKS, PIECE, WIDTH), jnp.bfloat16),
            pltpu.VMEM((4, 16, PIECE, WIDTH), jnp.bfloat16),
            pltpu.VMEM((4, 4, 128, 128), jnp.float32),
            pltpu.VMEM((4, 128, 128), jnp.float32),
            pltpu.VMEM((4, 128, 128), jnp.float32),
            pltpu.VMEM((2, 8, 128), jnp.float32),
            pltpu.VMEM((2, 8, 128), jnp.float32),
            pltpu.VMEM((4, 2, 128, 128), jnp.float32),
            pltpu.VMEM((4, 128, 128), jnp.bfloat16),
            pltpu.VMEM((4, 128, 128), jnp.bfloat16),
            dma,
            dma((2, RING)),
            dma((2, RING)),
            dma((4, 32)),
            dma((4, 8)),
            dma((6,)),
            dma((6,)),
        ],
        compiler_params=pltpu.CompilerParams(
            collective_id=0, has_side_effects=True, vmem_limit_bytes=32 * 1024 * 1024
        ),
        cost_estimate=pl.CostEstimate(
            flops=2 * 512 * 512 * 4096, bytes_accessed=1 << 20, transcendentals=0),
    )(grads.reshape(CHUNKS, PIECE, WIDTH))
    return out


def solution(mesh):
    return jax.shard_map(
        local,
        mesh=mesh,
        in_specs=(P("ex", "feat"),),
        out_specs=P("ex", "feat", None),
        check_vma=False,
    )
```

```python
import math

import jax
import jax.numpy as jnp
from jax import lax
from jax.experimental import pallas as pl
from jax.experimental.pallas import tpu as pltpu
from jax.sharding import PartitionSpec as P

MESH = pl.DeviceIdType.MESH
NZ = 16
ROWS = 128
WIDTH = 1024
CHUNKS = 4
PIECE = 32
RING = 30
RUN_RING = True
RUN_XY = True
RUN_MATH = True
P_TICKS = (16, 20, 21, 24, 25)
SQ_TICKS = (13, 17, 22, 26)
EVENTS = (
    (874972992, 744686276, 879171396, 740496064, 950478728, 753083084, 954677132, 748892872, 537734985, 10171660,
     541933389, 14361864, 546180993, 1774852, 550379397, 5965056),
    (143475139, 759367937, 147673543, 755177733, 68051403, 767764745, 72249807, 763574541, 272459009, 12270920,
     276657413, 16461132, 280904969, 3874176, 285103373, 8064388),
    (891823569, 550767628, 896021973, 546577416, 967312857, 542387204, 971511261, 538196992, 80749058, 135794958,
     76558854, 139985162, 139461130, 77082886, 135270926, 81273090),
    (489689226, 761479432, 493879438, 757289228, 498085954, 769876224, 502276166, 765686020, 12863323, 768944133,
     8673119, 764753921, 4482963, 760612877, 292759, 756422665),
    (6297099, 286266382, 2098703, 290456586, 14693891, 294663174, 10495495, 298853378, 11026511, 297795609,
     15224907, 293605405, 2646151, 289415185, 6844547, 285224981),
    (21128032, 7612943, 16937828, 3422731, 29442984, 15993351, 25252780, 11803139, 915411972, 7474694, 919602176,
     3284482, 974140428, 15805966, 978330632, 11615754),
    (7890401, 30118098, 3700197, 25919702, 16270825, 21737690, 12080621, 17539294, 288453646, 29064536, 292643850,
     33254748, 296899590, 20667792, 301089794, 24858004),
    (161494882, 567289107, 165685094, 563098903, 85989290, 558892315, 90179502, 554702111, 6316562, 558135298,
     2126358, 553936902, 14696986, 566515722, 10506782, 562317326),
    (23563276, 22249752, 19373064, 18059548, 31960068, 30646544, 27769856, 26456340, 30256135, 362828945, 26065923,
     367019157, 21924879, 421557337, 17734667, 425747549),
    (922768923, 303069926, 926959135, 307260130, 998274579, 311450350, 1002464791, 315640554, 570721375, 16819949,
     574919771, 21018345, 579118231, 25200357, 583316627, 29398753),
    (14852111, 296254475, 10661899, 300444687, 6389767, 287857667, 2199555, 292047879, 22040602, 154687788,
     17842206, 158877992, 30437394, 95975716, 26238998, 100165920),
    (579899889, 792747234, 584090101, 788548838, 571519481, 801144042, 575709693, 796945646, 114326393, 787849239,
     110127997, 783659027, 173038513, 779517983, 168840117, 775327771),
    (31311895, 26512428, 27121683, 30710824, 22997023, 18132004, 18806811, 22330400, 42502435, 316688427, 46700839,
     312498223, 34122027, 308308003, 38320431, 304117799),
    (523268266, 251961901, 527458478, 256160297, 531648610, 260342309, 535838822, 264540705, 934304790, 38962724,
     938494994, 34772512, 993033246, 47293996, 997223450, 43103784),
    (39365670, 49010725, 35175458, 44812321, 47746094, 40630317, 43555882, 36431913, 319929388, 60552554,
     324119592, 64742766, 328375332, 52155810, 332565536, 56346022),
    (31645727, 586181937, 27455515, 581991733, 23183383, 577785145, 18993171, 573594941, 37792304, 577040416,
     33602100, 572842020, 46172728, 585420840, 41982524, 581222444),
    (41477172, 41142570, 37286960, 36952366, 49857596, 49539362, 45667384, 45349158, 131119141, 394304675,
     126920737, 398494887, 189831213, 453033067, 185632809, 457223279),
    (46327853, 43306044, 42137641, 47504440, 37865509, 34925620, 33675297, 39124016, 59296051, 35712767, 63494455,
     39911163, 50915643, 44093175, 55114047, 48291571),
    (56159286, 55894589, 51969074, 51704377, 64539710, 64274997, 60349498, 60084785, 62954534, 186175806, 58756130,
     190366010, 54574126, 127463734, 50375722, 131653938),
    (57718831, 602975294, 53520427, 598785082, 66099239, 594578486, 61900835, 590388274, 60871807, 50718773,
     65062011, 54917169, 52491447, 59164733, 56681651, 63363129),
    (66121789, 59825466, 61923385, 64015678, 57724981, 51445042, 53526577, 55635254, 57735220, 58251443, 53536816,
     54053047, 66115644, 66648187, 61917240, 62449791),
    (62, 59, 58, 63, 54, 51, 50, 55, 54, 50, 50, 54, 62, 58, 58, 62),
)
DONE = (
    (21103364, 10551552, 21103364, 10551552, 21103364, 10551552, 21103364, 10551552, 4227200, 0, 4227200, 0,
     4227200, 0, 4227200, 0),
    (50661517, 40093064, 50661517, 40093064, 50661517, 40093064, 50661517, 40093064, 27411204, 29524739, 27411204,
     29524739, 27411204, 29524739, 27411204, 29524739),
    (84480028, 71798038, 84480028, 71798038, 84480028, 71798038, 84480028, 71798038, 57002384, 63343378, 57002384,
     63343378, 57002384, 63343378, 57002384, 63343378),
    (111974316, 105616678, 111974316, 105616678, 111974316, 105616678, 111974316, 105616678, 90821023, 97162018,
     90821023, 97162018, 90821023, 97162018, 90821023, 97162018),
    (128900408, 128883765, 128900408, 128883765, 128900408, 128883765, 128900408, 128883765, 120428847, 126786354,
     120428847, 126786354, 120428847, 126786354, 120428847, 126786354),
    (135274558, 135258046, 135274558, 135258046, 135274558, 135258046, 135274558, 135258046, 135257916, 135274559,
     135257916, 135274559, 135257916, 135274559, 135257916, 135274559),
    (135274560, 135274560, 135274560, 135274560, 135274560, 135274560, 135274560, 135274560, 135274560, 135274560,
     135274560, 135274560, 135274560, 135274560, 135274560, 135274560),
)


def kernel(
    g_ref, out_ref, cols, rows, acc, colsq, rowsq, sq_out, sq_in, swap_in, half_out, half_in,
    load_sem, ring_send, ring_recv, xy_send, xy_recv, tail_send, tail_recv,
):
    ex = lax.axis_index("ex")
    feat = lax.axis_index("feat")
    h, y, x = ex // 16, ex // 4 % 4, ex % 4
    l, c = feat // 2, feat % 2
    z = h * 4 + l
    big_y = y // 2
    dx = (x - l % 2 * 2 + 4) % 4
    dy = (y - l // 2 + 4) % 4

    def device(zz, yy, xx, cc):
        return (zz // 4 * 16 + yy * 4 + xx, zz % 4 * 2 + cc)

    z_up, z_down = device((z + 1) % NZ, y, x, c), device((z + NZ - 1) % NZ, y, x, c)
    plane = (
        device(z, y, (x + 1) % 4, c), device(z, y, (x + 3) % 4, c),
        device(z, (y + 1) % 4, x, c), device(z, (y + 3) % 4, x, c),
    )
    opposite = device(z, (y + 2) % 4, x, c)
    sibling = device(z, y, x, 1 - c)

    def remote(src, dst, send, recv, to):
        return pltpu.make_async_remote_copy(
            src_ref=src, dst_ref=dst, send_sem=send, recv_sem=recv, device_id=to,
            device_id_type=MESH,
        )

    load = pltpu.make_async_copy(g_ref, cols.at[z], load_sem)
    load.start()
    barrier = pltpu.get_barrier_semaphore()
    for to in (z_up, z_down, *plane, opposite, sibling):
        pl.semaphore_signal(barrier, inc=1, device_id=to, device_id_type=MESH)
    acc[...] = jnp.zeros_like(acc)
    colsq[...] = jnp.zeros_like(colsq)
    load.wait()
    pl.semaphore_wait(barrier, 8)

    def ring_copy(way, n, far):
        j = n % CHUNKS if way == 0 else CHUNKS - 1 - n % CHUNKS
        owner = (z - far + NZ) % NZ if way == 0 else (z + far) % NZ
        ref = cols.at[owner, j]
        to = z_up if way == 0 else z_down
        return remote(ref, ref, ring_send.at[way, n], ring_recv.at[way, n], to)

    def ring_start(n):
        for way in range(2):
            ring_copy(way, n, n // CHUNKS).start()

    def ring_round(n):
        for way in range(2):
            ring_copy(way, n, n // CHUNKS + 1).wait_recv()
            if n + CHUNKS < RING:
                ring_copy(way, n + CHUNKS, n // CHUNKS + 1).start()

    def ring_sent(n):
        for way in range(2):
            ring_copy(way, n, 0).wait_send()

    place = dx * 4 + dy
    source = (dx < 2) & (dy % 2 == 0)

    def here(table):
        value = jnp.int32(table[0])
        for index, entry in enumerate(table[1:], 1):
            value = jnp.where(place == index, jnp.int32(entry), value)
        return value

    events = [here(table) for table in EVENTS]
    done = [here(table) for table in DONE]
    handled = [jnp.int32(0)] + [done[n // 4] // 128 ** (n % 4) % 128 for n in range(28)]

    def slice_of(k):
        return (l // 2 + k // 2) % 2 * 2 + (l + k) % 2

    def row_piece(k, q):
        part = q % 4
        part = jnp.where(slice_of(k) > l, 3 - part, part)
        return rows.at[slice_of(k), q // 4 * 4 + part]

    def set_out(k, part):
        @pl.when(source)
        def _():
            q = 4 * (2 * dx + dy // 2) + part
            chunk = jnp.where(slice_of(k) > l, 3 - part, part)
            pltpu.make_async_copy(
                cols.at[h * 4 + slice_of(k), chunk], row_piece(k, q), xy_recv.at[k, q]).start()

    def decoded(e):
        third = e // 3
        word = events[0]
        for index in range(1, len(events)):
            word = jnp.where(third == index, events[index], word)
        digit = jnp.right_shift(word, (e - third * 3) * 10)
        return digit // 16 % 4, digit % 16, [digit // (64 * 2**d) % 2 == 1 for d in range(4)]

    def onward(k, q, d):
        ref = row_piece(k, q)
        return remote(ref, ref, xy_send.at[k, 4 * q + d], xy_recv.at[k, q], plane[d])

    def take(e, carry):
        k, q, goes = decoded(e)
        onward(k, q, 0).wait_recv()
        for d in range(4):
            pl.when(goes[d])(onward(k, q, d).start)
        return carry

    def take_until(n):
        lax.fori_loop(handled[n], handled[n + 1], take, 0)

    def xy_sent(start, stop):
        def body(e, carry):
            k, q, goes = decoded(e)
            for d in range(4):
                pl.when(goes[d])(onward(k, q, d).wait_send)
            return carry

        lax.fori_loop(start, stop, body, 0)

    def squares(block):
        wide = block.astype(jnp.float32)
        wide = wide * wide
        total = wide[:, :128]
        for part in range(1, WIDTH // 128):
            total = total + wide[:, part * 128:part * 128 + 128]
        return total

    def cube(b):
        return (h + b + b // 2 - b // 3 * 2) % 4

    def multiply(b, k):
        ll = slice_of(k)
        block = cols[cube(b) * 4 + ll].reshape(ROWS, WIDTH)
        product = lax.dot_general(
            rows[ll].reshape(4 * ROWS, WIDTH), block, (((1,), (1,)), ((), ())),
            preferred_element_type=jnp.float32,
        )
        acc[b] += product.reshape(4, ROWS, 128)
        colsq[b] += squares(block)

    def multiply_all(k, blocks):
        def body(i, carry):
            b = blocks[0]
            for index in range(1, len(blocks)):
                b = jnp.where(i == index, blocks[index], b)
            multiply(b % 4, k)
            return carry

        lax.fori_loop(0, len(blocks), body, 0)

    def row_squares(k):
        ll = slice_of(k)

        def body(i, carry):
            total = squares(rows[ll, pl.ds(4 * i, 4)].reshape(ROWS, WIDTH))
            if k:
                total = total + rowsq[i]
            rowsq[i] = total
            return carry

        lax.fori_loop(0, 4, body, 0)

    eye = lax.broadcasted_iota(jnp.int32, (128, 128), 0) == lax.broadcasted_iota(
        jnp.int32, (128, 128), 1)

    def to_lanes(folded):
        column = jnp.sum(folded, axis=1, keepdims=True)
        return jnp.sum(jnp.where(eye, column, 0.0), axis=0, keepdims=True)

    def to_rows(lanes):
        return jnp.sum(jnp.where(eye, lanes, 0.0), axis=1, keepdims=True)

    last = jnp.where(l == 0, 1, jnp.where(l == 3, 2, 3))

    far = jnp.where(l < 2, 1, 2)
    plan = {
        P_TICKS[0]: lambda: multiply_all(0, (0, 1, 2)),
        P_TICKS[1]: lambda: multiply_all(1, (0, 1, 2)),
        P_TICKS[2]: lambda: multiply_all(2, (0, 3 - far)),
        P_TICKS[3]: lambda: multiply_all(2, (far, 3)),
        P_TICKS[4]: lambda: multiply_all(3, (last + 1, last + 2, last + 3)),
    }
    if RUN_RING:
        for n in range(CHUNKS):
            ring_start(n)
    for tick in range(28):
        if RUN_XY:
            if tick == 0:
                for part in range(4):
                    set_out(0, part)
            elif tick <= 3 * CHUNKS:
                set_out(1 + (tick - 1) // CHUNKS, (tick - 1) % CHUNKS)
            take_until(tick)
        if RUN_MATH:
            if tick in SQ_TICKS:
                row_squares(SQ_TICKS.index(tick))
            if tick in plan:
                plan[tick]()
        if RUN_RING:
            ring_round(tick)
            if tick >= 8:
                ring_sent(tick - 8)
        if RUN_XY and tick >= 16:
            xy_sent(handled[tick - 8] if tick > 16 else 0, handled[tick - 7])

    def settle():
        if RUN_XY:
            xy_sent(handled[20], 64)
        if RUN_RING:
            for n in range(20, RING):
                ring_sent(n)

    other = 1 - c
    if RUN_MATH:
        multiply(3, 1)
        multiply(last, 3)
        for b in range(3):
            sq_out[0, b:b + 1] = to_lanes(colsq[b])
        for p in range(4):
            sq_out[0, 4 + p:5 + p] = to_lanes(rowsq[p])
        swaps = [
            remote(sq_out.at[0], sq_in.at[0], tail_send.at[0], tail_recv.at[0], sibling),
            remote(
                acc.at[pl.ds(0, 3), pl.ds(2 * other, 2)], swap_in.at[pl.ds(0, 3)], tail_send.at[1],
                tail_recv.at[1], sibling),
            remote(sq_out.at[1], sq_in.at[1], tail_send.at[2], tail_recv.at[2], sibling),
            remote(
                acc.at[3, pl.ds(2 * other, 2)], swap_in.at[3], tail_send.at[3], tail_recv.at[3],
                sibling),
        ]
        swaps[0].start()
        swaps[1].start()

    if RUN_RING:
        for n in range(28, RING):
            ring_round(n)

    if RUN_MATH:
        multiply(3, 0)
        sq_out[1] = jnp.broadcast_to(to_lanes(colsq[3]), (8, 128))
        swaps[2].start()
        swaps[3].start()
        swaps[0].wait()
        scales = lax.rsqrt(sq_out[0] + sq_in[0] + 1e-6)
        swaps[1].wait()
        row_scale = [
            to_rows(jnp.where(c == 0, scales[4 + yy:5 + yy], scales[6 + yy:7 + yy]))
            for yy in range(2)
        ]
        row_here = jnp.where(big_y == 0, row_scale[0], row_scale[1])
        row_there = jnp.where(big_y == 0, row_scale[1], row_scale[0])

        def result(b, yy, row_side, col_side):
            raw = acc[b, 2 * c + yy] + swap_in[b, yy]
            value = raw * row_side * (col_side * math.sqrt(8192.0))
            return jnp.where((row_side > 0.0) & (col_side > 0.0), value, 0.0)

        for b in range(3):
            half_out[b] = result(b, 1 - big_y, row_there, scales[b:b + 1]).astype(jnp.bfloat16)
        across = [
            remote(
                half_out.at[pl.ds(0, 3)], half_in.at[pl.ds(0, 3)], tail_send.at[4],
                tail_recv.at[4], opposite),
            remote(half_out.at[3], half_in.at[3], tail_send.at[5], tail_recv.at[5], opposite),
        ]
        across[0].start()
        swaps[2].wait()
        scale = lax.rsqrt(sq_out[1] + sq_in[1] + 1e-6)[:1]
        swaps[3].wait()
        half_out[3] = result(3, 1 - big_y, row_there, scale).astype(jnp.bfloat16)
        across[1].start()

        def store(b, yy, value):
            at = pl.multiple_of((2 * cube(b) + yy) * 128, 128)
            out_ref[0, :, pl.ds(at, 128)] = value

        for b in range(4):
            value = result(b, big_y, row_here, scales[b:b + 1] if b < 3 else scale)
            if b == 0:
                value = jnp.where(eye & (2 * l + c == ex % 8), 0.0, value)
            store(b, big_y, value)
        settle()
        across[0].wait()
        for b in range(3):
            store(b, 1 - big_y, half_in[b].astype(jnp.float32))
        across[1].wait()
        store(3, 1 - big_y, half_in[3].astype(jnp.float32))
    else:
        out_ref[...] = jnp.zeros_like(out_ref)
        settle()


def local(grads):
    dma = pltpu.SemaphoreType.DMA
    out = pl.pallas_call(
        kernel,
        out_shape=jax.ShapeDtypeStruct((1, 128, 1024), jnp.float32),
        in_specs=[pl.BlockSpec(memory_space=pl.ANY)],
        out_specs=pl.BlockSpec(memory_space=pltpu.VMEM),
        scratch_shapes=[
            pltpu.VMEM((NZ, CHUNKS, PIECE, WIDTH), jnp.bfloat16),
            pltpu.VMEM((4, 16, PIECE, WIDTH), jnp.bfloat16),
            pltpu.VMEM((4, 4, 128, 128), jnp.float32),
            pltpu.VMEM((4, 128, 128), jnp.float32),
            pltpu.VMEM((4, 128, 128), jnp.float32),
            pltpu.VMEM((2, 8, 128), jnp.float32),
            pltpu.VMEM((2, 8, 128), jnp.float32),
            pltpu.VMEM((4, 2, 128, 128), jnp.float32),
            pltpu.VMEM((4, 128, 128), jnp.bfloat16),
            pltpu.VMEM((4, 128, 128), jnp.bfloat16),
            dma,
            dma((2, RING)),
            dma((2, RING)),
            dma((4, 64)),
            dma((4, 16)),
            dma((6,)),
            dma((6,)),
        ],
        compiler_params=pltpu.CompilerParams(
            collective_id=0, has_side_effects=True, vmem_limit_bytes=32 * 1024 * 1024
        ),
        cost_estimate=pl.CostEstimate(
            flops=2 * 512 * 512 * 4096, bytes_accessed=1 << 20, transcendentals=0),
    )(pltpu.with_memory_space_constraint(grads.reshape(CHUNKS, PIECE, WIDTH), pltpu.HBM))
    return out


def solution(mesh):
    return jax.shard_map(
        local,
        mesh=mesh,
        in_specs=(P("ex", "feat"),),
        out_specs=P("ex", "feat", None),
        check_vma=False,
    )
```

```python
import math

import jax
import jax.numpy as jnp
from jax import lax
from jax.experimental import pallas as pl
from jax.experimental.pallas import tpu as pltpu
from jax.sharding import PartitionSpec as P

MESH = pl.DeviceIdType.MESH
NZ = 16
ROWS = 128
WIDTH = 1024
CHUNKS = 4
PIECE = 32
RING = 30
EVENTS = (
    (874972992, 744686276, 879171396, 740496064, 950478728, 753083084, 954677132, 748892872, 537734985, 10171660,
     541933389, 14361864, 546180993, 1774852, 550379397, 5965056),
    (143475139, 759367937, 147673543, 755177733, 68051403, 767764745, 72249807, 763574541, 272459009, 12270920,
     276657413, 16461132, 280904969, 3874176, 285103373, 8064388),
    (891823569, 550767628, 896021973, 546577416, 967312857, 542387204, 971511261, 538196992, 80749058, 135794958,
     76558854, 139985162, 139461130, 77082886, 135270926, 81273090),
    (489689226, 761479432, 493879438, 757289228, 498085954, 769876224, 502276166, 765686020, 12863323, 768944133,
     8673119, 764753921, 4482963, 760612877, 292759, 756422665),
    (6297099, 286266382, 2098703, 290456586, 14693891, 294663174, 10495495, 298853378, 11026511, 297795609,
     15224907, 293605405, 2646151, 289415185, 6844547, 285224981),
    (21128032, 7612943, 16937828, 3422731, 29442984, 15993351, 25252780, 11803139, 915411972, 7474694, 919602176,
     3284482, 974140428, 15805966, 978330632, 11615754),
    (7890401, 30118098, 3700197, 25919702, 16270825, 21737690, 12080621, 17539294, 288453646, 29064536, 292643850,
     33254748, 296899590, 20667792, 301089794, 24858004),
    (161494882, 567289107, 165685094, 563098903, 85989290, 558892315, 90179502, 554702111, 6316562, 558135298,
     2126358, 553936902, 14696986, 566515722, 10506782, 562317326),
    (23563276, 22249752, 19373064, 18059548, 31960068, 30646544, 27769856, 26456340, 30256135, 362828945, 26065923,
     367019157, 21924879, 421557337, 17734667, 425747549),
    (922768923, 303069926, 926959135, 307260130, 998274579, 311450350, 1002464791, 315640554, 570721375, 16819949,
     574919771, 21018345, 579118231, 25200357, 583316627, 29398753),
    (14852111, 296254475, 10661899, 300444687, 6389767, 287857667, 2199555, 292047879, 22040602, 154687788,
     17842206, 158877992, 30437394, 95975716, 26238998, 100165920),
    (579899889, 792747234, 584090101, 788548838, 571519481, 801144042, 575709693, 796945646, 114326393, 787849239,
     110127997, 783659027, 173038513, 779517983, 168840117, 775327771),
    (31311895, 26512428, 27121683, 30710824, 22997023, 18132004, 18806811, 22330400, 42502435, 316688427, 46700839,
     312498223, 34122027, 308308003, 38320431, 304117799),
    (523268266, 251961901, 527458478, 256160297, 531648610, 260342309, 535838822, 264540705, 934304790, 38962724,
     938494994, 34772512, 993033246, 47293996, 997223450, 43103784),
    (39365670, 49010725, 35175458, 44812321, 47746094, 40630317, 43555882, 36431913, 319929388, 60552554,
     324119592, 64742766, 328375332, 52155810, 332565536, 56346022),
    (31645727, 586181937, 27455515, 581991733, 23183383, 577785145, 18993171, 573594941, 37792304, 577040416,
     33602100, 572842020, 46172728, 585420840, 41982524, 581222444),
    (41477172, 41142570, 37286960, 36952366, 49857596, 49539362, 45667384, 45349158, 131119141, 394304675,
     126920737, 398494887, 189831213, 453033067, 185632809, 457223279),
    (46327853, 43306044, 42137641, 47504440, 37865509, 34925620, 33675297, 39124016, 59296051, 35712767, 63494455,
     39911163, 50915643, 44093175, 55114047, 48291571),
    (56159286, 55894589, 51969074, 51704377, 64539710, 64274997, 60349498, 60084785, 62954534, 186175806, 58756130,
     190366010, 54574126, 127463734, 50375722, 131653938),
    (57718831, 602975294, 53520427, 598785082, 66099239, 594578486, 61900835, 590388274, 60871807, 50718773,
     65062011, 54917169, 52491447, 59164733, 56681651, 63363129),
    (66121789, 59825466, 61923385, 64015678, 57724981, 51445042, 53526577, 55635254, 57735220, 58251443, 53536816,
     54053047, 66115644, 66648187, 61917240, 62449791),
    (62, 59, 58, 63, 54, 51, 50, 55, 54, 50, 50, 54, 62, 58, 58, 62),
)
DONE = (
    (21103364, 10551552, 21103364, 10551552, 21103364, 10551552, 21103364, 10551552, 4227200, 0, 4227200, 0,
     4227200, 0, 4227200, 0),
    (50661517, 40093064, 50661517, 40093064, 50661517, 40093064, 50661517, 40093064, 27411204, 29524739, 27411204,
     29524739, 27411204, 29524739, 27411204, 29524739),
    (84480028, 71798038, 84480028, 71798038, 84480028, 71798038, 84480028, 71798038, 57002384, 63343378, 57002384,
     63343378, 57002384, 63343378, 57002384, 63343378),
    (111974316, 105616678, 111974316, 105616678, 111974316, 105616678, 111974316, 105616678, 90821023, 97162018,
     90821023, 97162018, 90821023, 97162018, 90821023, 97162018),
    (128900408, 128883765, 128900408, 128883765, 128900408, 128883765, 128900408, 128883765, 120428847, 126786354,
     120428847, 126786354, 120428847, 126786354, 120428847, 126786354),
    (135274558, 135258046, 135274558, 135258046, 135274558, 135258046, 135274558, 135258046, 135257916, 135274559,
     135257916, 135274559, 135257916, 135274559, 135257916, 135274559),
    (135274560, 135274560, 135274560, 135274560, 135274560, 135274560, 135274560, 135274560, 135274560, 135274560,
     135274560, 135274560, 135274560, 135274560, 135274560, 135274560),
)


def kernel(
    g_ref, out_ref, cols, rows, acc, colsq, rowsq, sq_out, sq_in, swap_in, half_out, half_in,
    load_sem, ring_send, ring_recv, xy_send, xy_recv, tail_send, tail_recv,
):
    ex = lax.axis_index("ex")
    feat = lax.axis_index("feat")
    h, y, x = ex // 16, ex // 4 % 4, ex % 4
    l, c = feat // 2, feat % 2
    z = h * 4 + l
    big_y = y // 2
    dx = (x - l % 2 * 2 + 4) % 4
    dy = (y - l // 2 + 4) % 4

    def device(zz, yy, xx, cc):
        return (zz // 4 * 16 + yy * 4 + xx, zz % 4 * 2 + cc)

    z_up, z_down = device((z + 1) % NZ, y, x, c), device((z + NZ - 1) % NZ, y, x, c)
    plane = (
        device(z, y, (x + 1) % 4, c), device(z, y, (x + 3) % 4, c),
        device(z, (y + 1) % 4, x, c), device(z, (y + 3) % 4, x, c),
    )
    opposite = device(z, (y + 2) % 4, x, c)
    sibling = device(z, y, x, 1 - c)

    def remote(src, dst, send, recv, to):
        return pltpu.make_async_remote_copy(
            src_ref=src, dst_ref=dst, send_sem=send, recv_sem=recv, device_id=to,
            device_id_type=MESH,
        )

    load = pltpu.make_async_copy(g_ref, cols.at[z], load_sem)
    load.start()
    barrier = pltpu.get_barrier_semaphore()
    for to in (z_up, z_down, *plane, opposite, sibling):
        pl.semaphore_signal(barrier, inc=1, device_id=to, device_id_type=MESH)
    acc[...] = jnp.zeros_like(acc)
    colsq[...] = jnp.zeros_like(colsq)
    place = dx * 4 + dy
    source = (dx < 2) & (dy % 2 == 0)

    def here(table):
        value = jnp.int32(table[0])
        for index, entry in enumerate(table[1:], 1):
            value = jnp.where(place == index, jnp.int32(entry), value)
        return value

    events = [here(table) for table in EVENTS]
    done = [here(table) for table in DONE]
    handled = [jnp.int32(0)] + [done[n // 4] // 128 ** (n % 4) % 128 for n in range(28)]

    load.wait()
    pl.semaphore_wait(barrier, 8)

    def ring_copy(way, n, far):
        j = n % CHUNKS if way == 0 else CHUNKS - 1 - n % CHUNKS
        owner = (z - far + NZ) % NZ if way == 0 else (z + far) % NZ
        ref = cols.at[owner, j]
        to = z_up if way == 0 else z_down
        return remote(ref, ref, ring_send.at[way, n], ring_recv.at[way, n], to)

    def ring_start(n):
        for way in range(2):
            ring_copy(way, n, n // CHUNKS).start()

    def ring_round(n):
        for way in range(2):
            ring_copy(way, n, n // CHUNKS + 1).wait_recv()
            if n + CHUNKS < RING:
                ring_copy(way, n + CHUNKS, n // CHUNKS + 1).start()

    def ring_sent(n):
        for way in range(2):
            ring_copy(way, n, 0).wait_send()

    for n in range(CHUNKS):
        ring_start(n)

    def slice_of(k):
        return (l // 2 + k // 2) % 2 * 2 + (l + k) % 2

    def row_piece(k, q):
        part = q % 4
        part = jnp.where(slice_of(k) > l, 3 - part, part)
        return rows.at[slice_of(k), q // 4 * 4 + part]

    def set_out(k, part):
        @pl.when(source)
        def _():
            q = 4 * (2 * dx + dy // 2) + part
            chunk = jnp.where(slice_of(k) > l, 3 - part, part)
            pltpu.make_async_copy(
                cols.at[h * 4 + slice_of(k), chunk], row_piece(k, q), xy_recv.at[k, q]).start()

    def decoded(e):
        third = e // 3
        word = events[0]
        for index in range(1, len(events)):
            word = jnp.where(third == index, events[index], word)
        digit = jnp.right_shift(word, (e - third * 3) * 10)
        return digit // 16 % 4, digit % 16, [digit // (64 * 2**d) % 2 == 1 for d in range(4)]

    def onward(k, q, d):
        ref = row_piece(k, q)
        return remote(ref, ref, xy_send.at[k, 4 * q + d], xy_recv.at[k, q], plane[d])

    def take(e, carry):
        k, q, goes = decoded(e)
        onward(k, q, 0).wait_recv()
        for d in range(4):
            pl.when(goes[d])(onward(k, q, d).start)
        return carry

    def take_until(n):
        lax.fori_loop(handled[n], handled[n + 1], take, 0)

    def xy_sent(start, stop):
        def body(e, carry):
            k, q, goes = decoded(e)
            for d in range(4):
                pl.when(goes[d])(onward(k, q, d).wait_send)
            return carry

        lax.fori_loop(start, stop, body, 0)

    def squares(block):
        wide = block.astype(jnp.float32)
        wide = wide * wide
        total = wide[:, :128]
        for part in range(1, WIDTH // 128):
            total = total + wide[:, part * 128:part * 128 + 128]
        return total

    def cube(b):
        return (h + b + b // 2 - b // 3 * 2) % 4

    def multiply(b, k):
        ll = slice_of(k)
        block = cols[cube(b) * 4 + ll].reshape(ROWS, WIDTH)
        product = lax.dot_general(
            rows[ll].reshape(4 * ROWS, WIDTH), block, (((1,), (1,)), ((), ())),
            preferred_element_type=jnp.float32,
        )
        acc[b] += product.reshape(4, ROWS, 128)
        colsq[b] += squares(block)

    def row_squares(k):
        ll = slice_of(k)

        def body(i, carry):
            total = squares(rows[ll, pl.ds(4 * i, 4)].reshape(ROWS, WIDTH))
            if k:
                total = total + rowsq[i]
            rowsq[i] = total
            return carry

        lax.fori_loop(0, 4, body, 0)

    eye = lax.broadcasted_iota(jnp.int32, (128, 128), 0) == lax.broadcasted_iota(
        jnp.int32, (128, 128), 1)

    def to_lanes(folded):
        column = jnp.sum(folded, axis=1, keepdims=True)
        return jnp.sum(jnp.where(eye, column, 0.0), axis=0, keepdims=True)

    def to_rows(lanes):
        return jnp.sum(jnp.where(eye, lanes, 0.0), axis=1, keepdims=True)

    last = jnp.where(l == 0, 1, jnp.where(l == 3, 2, 3))

    far = jnp.where(l < 2, 1, 2)
    near = 3 - far
    products = {
        12: [(0, 0)], 16: [(1, 0)], 17: [(2, 0)], 18: [(0, 1)], 20: [(1, 1)], 21: [(2, 1)], 22: [(0, 2)],
        23: [(near, 2)], 24: [(far, 2)], 25: [(3, 2)],
        26: [((last + 1) % 4, 3), ((last + 2) % 4, 3), ((last + 3) % 4, 3)],
    }
    row_sums = {13: 0, 19: 1, 24: 2, 26: 3}
    for tick in range(28):
        if tick == 0:
            for part in range(4):
                set_out(0, part)
        elif tick <= 3 * CHUNKS:
            set_out(1 + (tick - 1) // CHUNKS, (tick - 1) % CHUNKS)
        take_until(tick)
        if tick in row_sums:
            row_squares(row_sums[tick])
        for b, k in products.get(tick, ()):
            multiply(b, k)
        ring_round(tick)
        if tick >= 8:
            ring_sent(tick - 8)
        if tick >= 16:
            xy_sent(handled[tick - 8] if tick > 16 else 0, handled[tick - 7])

    def settle():
        xy_sent(handled[20], 64)
        for n in range(20, RING):
            ring_sent(n)

    other = 1 - c
    multiply(3, 1)
    multiply(last, 3)
    for b in range(3):
        sq_out[0, b:b + 1] = to_lanes(colsq[b])
    for p in range(4):
        sq_out[0, 4 + p:5 + p] = to_lanes(rowsq[p])
    swaps = [
        remote(sq_out.at[0], sq_in.at[0], tail_send.at[0], tail_recv.at[0], sibling),
        remote(
            acc.at[pl.ds(0, 3), pl.ds(2 * other, 2)], swap_in.at[pl.ds(0, 3)], tail_send.at[1],
            tail_recv.at[1], sibling),
        remote(sq_out.at[1], sq_in.at[1], tail_send.at[2], tail_recv.at[2], sibling),
        remote(
            acc.at[3, pl.ds(2 * other, 2)], swap_in.at[3], tail_send.at[3], tail_recv.at[3],
            sibling),
    ]
    swaps[0].start()
    swaps[1].start()

    for n in range(28, RING):
        ring_round(n)

    multiply(3, 0)
    sq_out[1] = jnp.broadcast_to(to_lanes(colsq[3]), (8, 128))
    swaps[2].start()
    swaps[3].start()
    swaps[0].wait()
    scales = lax.rsqrt(sq_out[0] + sq_in[0] + 1e-6)
    swaps[1].wait()
    row_scale = [
        to_rows(jnp.where(c == 0, scales[4 + yy:5 + yy], scales[6 + yy:7 + yy]))
        for yy in range(2)
    ]
    row_here = jnp.where(big_y == 0, row_scale[0], row_scale[1])
    row_there = jnp.where(big_y == 0, row_scale[1], row_scale[0])

    def result(b, yy, row_side, col_side):
        raw = acc[b, 2 * c + yy] + swap_in[b, yy]
        value = raw * row_side * (col_side * math.sqrt(8192.0))
        return jnp.where((row_side > 0.0) & (col_side > 0.0), value, 0.0)

    for b in range(3):
        half_out[b] = result(b, 1 - big_y, row_there, scales[b:b + 1]).astype(jnp.bfloat16)
    across = [
        remote(
            half_out.at[pl.ds(0, 3)], half_in.at[pl.ds(0, 3)], tail_send.at[4],
            tail_recv.at[4], opposite),
        remote(half_out.at[3], half_in.at[3], tail_send.at[5], tail_recv.at[5], opposite),
    ]
    across[0].start()
    swaps[2].wait()
    scale = lax.rsqrt(sq_out[1] + sq_in[1] + 1e-6)[:1]
    swaps[3].wait()
    half_out[3] = result(3, 1 - big_y, row_there, scale).astype(jnp.bfloat16)
    across[1].start()

    def store(b, yy, value):
        at = pl.multiple_of((2 * cube(b) + yy) * 128, 128)
        out_ref[0, :, pl.ds(at, 128)] = value

    for b in range(4):
        value = result(b, big_y, row_here, scales[b:b + 1] if b < 3 else scale)
        if b == 0:
            value = jnp.where(eye & (2 * l + c == ex % 8), 0.0, value)
        store(b, big_y, value)
    settle()
    across[0].wait()
    for b in range(3):
        store(b, 1 - big_y, half_in[b].astype(jnp.float32))
    across[1].wait()
    store(3, 1 - big_y, half_in[3].astype(jnp.float32))
def local(grads):
    dma = pltpu.SemaphoreType.DMA
    out = pl.pallas_call(
        kernel,
        out_shape=jax.ShapeDtypeStruct((1, 128, 1024), jnp.float32),
        in_specs=[pl.BlockSpec(memory_space=pl.ANY)],
        out_specs=pl.BlockSpec(memory_space=pltpu.VMEM),
        scratch_shapes=[
            pltpu.VMEM((NZ, CHUNKS, PIECE, WIDTH), jnp.bfloat16),
            pltpu.VMEM((4, 16, PIECE, WIDTH), jnp.bfloat16),
            pltpu.VMEM((4, 4, 128, 128), jnp.float32),
            pltpu.VMEM((4, 128, 128), jnp.float32),
            pltpu.VMEM((4, 128, 128), jnp.float32),
            pltpu.VMEM((2, 8, 128), jnp.float32),
            pltpu.VMEM((2, 8, 128), jnp.float32),
            pltpu.VMEM((4, 2, 128, 128), jnp.float32),
            pltpu.VMEM((4, 128, 128), jnp.bfloat16),
            pltpu.VMEM((4, 128, 128), jnp.bfloat16),
            dma,
            dma((2, RING)),
            dma((2, RING)),
            dma((4, 64)),
            dma((4, 16)),
            dma((6,)),
            dma((6,)),
        ],
        compiler_params=pltpu.CompilerParams(
            collective_id=0, has_side_effects=True, vmem_limit_bytes=32 * 1024 * 1024
        ),
        cost_estimate=pl.CostEstimate(
            flops=2 * 512 * 512 * 4096, bytes_accessed=1 << 20, transcendentals=0),
    )(pltpu.with_memory_space_constraint(grads.reshape(CHUNKS, PIECE, WIDTH), pltpu.HBM))
    return out


def solution(mesh):
    return jax.shard_map(
        local,
        mesh=mesh,
        in_specs=(P("ex", "feat"),),
        out_specs=P("ex", "feat", None),
        check_vma=False,
    )
```

```python
import math

import jax
import jax.numpy as jnp
from jax import lax
from jax.experimental import pallas as pl
from jax.experimental.pallas import tpu as pltpu
from jax.sharding import PartitionSpec as P

MESH = pl.DeviceIdType.MESH
NZ = 16
ROWS = 128
WIDTH = 1024
CHUNKS = 4
PIECE = 32
RING = 30
EVENTS = (
    (874972992, 744686276, 879171396, 740496064, 950478728, 753083084, 954677132, 748892872, 537734985, 10171660,
     541933389, 14361864, 546180993, 1774852, 550379397, 5965056),
    (143475139, 759367937, 147673543, 755177733, 68051403, 767764745, 72249807, 763574541, 272459009, 12270920,
     276657413, 16461132, 280904969, 3874176, 285103373, 8064388),
    (891823569, 550767628, 896021973, 546577416, 967312857, 542387204, 971511261, 538196992, 80749058, 135794958,
     76558854, 139985162, 139461130, 77082886, 135270926, 81273090),
    (489689226, 761479432, 493879438, 757289228, 498085954, 769876224, 502276166, 765686020, 12863323, 768944133,
     8673119, 764753921, 4482963, 760612877, 292759, 756422665),
    (6297099, 286266382, 2098703, 290456586, 14693891, 294663174, 10495495, 298853378, 11026511, 297795609,
     15224907, 293605405, 2646151, 289415185, 6844547, 285224981),
    (21128032, 7612943, 16937828, 3422731, 29442984, 15993351, 25252780, 11803139, 915411972, 7474694, 919602176,
     3284482, 974140428, 15805966, 978330632, 11615754),
    (7890401, 30118098, 3700197, 25919702, 16270825, 21737690, 12080621, 17539294, 288453646, 29064536, 292643850,
     33254748, 296899590, 20667792, 301089794, 24858004),
    (161494882, 567289107, 165685094, 563098903, 85989290, 558892315, 90179502, 554702111, 6316562, 558135298,
     2126358, 553936902, 14696986, 566515722, 10506782, 562317326),
    (23563276, 22249752, 19373064, 18059548, 31960068, 30646544, 27769856, 26456340, 30256135, 362828945, 26065923,
     367019157, 21924879, 421557337, 17734667, 425747549),
    (922768923, 303069926, 926959135, 307260130, 998274579, 311450350, 1002464791, 315640554, 570721375, 16819949,
     574919771, 21018345, 579118231, 25200357, 583316627, 29398753),
    (14852111, 296254475, 10661899, 300444687, 6389767, 287857667, 2199555, 292047879, 22040602, 154687788,
     17842206, 158877992, 30437394, 95975716, 26238998, 100165920),
    (579899889, 792747234, 584090101, 788548838, 571519481, 801144042, 575709693, 796945646, 114326393, 787849239,
     110127997, 783659027, 173038513, 779517983, 168840117, 775327771),
    (31311895, 26512428, 27121683, 30710824, 22997023, 18132004, 18806811, 22330400, 42502435, 316688427, 46700839,
     312498223, 34122027, 308308003, 38320431, 304117799),
    (523268266, 251961901, 527458478, 256160297, 531648610, 260342309, 535838822, 264540705, 934304790, 38962724,
     938494994, 34772512, 993033246, 47293996, 997223450, 43103784),
    (39365670, 49010725, 35175458, 44812321, 47746094, 40630317, 43555882, 36431913, 319929388, 60552554,
     324119592, 64742766, 328375332, 52155810, 332565536, 56346022),
    (31645727, 586181937, 27455515, 581991733, 23183383, 577785145, 18993171, 573594941, 37792304, 577040416,
     33602100, 572842020, 46172728, 585420840, 41982524, 581222444),
    (41477172, 41142570, 37286960, 36952366, 49857596, 49539362, 45667384, 45349158, 131119141, 394304675,
     126920737, 398494887, 189831213, 453033067, 185632809, 457223279),
    (46327853, 43306044, 42137641, 47504440, 37865509, 34925620, 33675297, 39124016, 59296051, 35712767, 63494455,
     39911163, 50915643, 44093175, 55114047, 48291571),
    (56159286, 55894589, 51969074, 51704377, 64539710, 64274997, 60349498, 60084785, 62954534, 186175806, 58756130,
     190366010, 54574126, 127463734, 50375722, 131653938),
    (57718831, 602975294, 53520427, 598785082, 66099239, 594578486, 61900835, 590388274, 60871807, 50718773,
     65062011, 54917169, 52491447, 59164733, 56681651, 63363129),
    (66121789, 59825466, 61923385, 64015678, 57724981, 51445042, 53526577, 55635254, 57735220, 58251443, 53536816,
     54053047, 66115644, 66648187, 61917240, 62449791),
    (62, 59, 58, 63, 54, 51, 50, 55, 54, 50, 50, 54, 62, 58, 58, 62),
)
DONE = (
    (21103364, 10551552, 21103364, 10551552, 21103364, 10551552, 21103364, 10551552, 4227200, 0, 4227200, 0,
     4227200, 0, 4227200, 0),
    (50661517, 40093064, 50661517, 40093064, 50661517, 40093064, 50661517, 40093064, 27411204, 29524739, 27411204,
     29524739, 27411204, 29524739, 27411204, 29524739),
    (84480028, 71798038, 84480028, 71798038, 84480028, 71798038, 84480028, 71798038, 57002384, 63343378, 57002384,
     63343378, 57002384, 63343378, 57002384, 63343378),
    (111974316, 105616678, 111974316, 105616678, 111974316, 105616678, 111974316, 105616678, 90821023, 97162018,
     90821023, 97162018, 90821023, 97162018, 90821023, 97162018),
    (128900408, 128883765, 128900408, 128883765, 128900408, 128883765, 128900408, 128883765, 120428847, 126786354,
     120428847, 126786354, 120428847, 126786354, 120428847, 126786354),
    (135274558, 135258046, 135274558, 135258046, 135274558, 135258046, 135274558, 135258046, 135257916, 135274559,
     135257916, 135274559, 135257916, 135274559, 135257916, 135274559),
    (135274560, 135274560, 135274560, 135274560, 135274560, 135274560, 135274560, 135274560, 135274560, 135274560,
     135274560, 135274560, 135274560, 135274560, 135274560, 135274560),
)


def kernel(
    g_ref, out_ref, cols, rows, acc, colsq, rowsq, sq_out, sq_in, swap_in, half_out, half_in,
    load_sem, ring_send, ring_recv, xy_send, xy_recv, tail_send, tail_recv,
):
    ex = lax.axis_index("ex")
    feat = lax.axis_index("feat")
    h, y, x = ex // 16, ex // 4 % 4, ex % 4
    l, c = feat // 2, feat % 2
    z = h * 4 + l
    big_y = y // 2
    dx = (x - l % 2 * 2 + 4) % 4
    dy = (y - l // 2 + 4) % 4

    def device(zz, yy, xx, cc):
        return (zz // 4 * 16 + yy * 4 + xx, zz % 4 * 2 + cc)

    z_up, z_down = device((z + 1) % NZ, y, x, c), device((z + NZ - 1) % NZ, y, x, c)
    plane = (
        device(z, y, (x + 1) % 4, c), device(z, y, (x + 3) % 4, c),
        device(z, (y + 1) % 4, x, c), device(z, (y + 3) % 4, x, c),
    )
    opposite = device(z, (y + 2) % 4, x, c)
    sibling = device(z, y, x, 1 - c)

    def remote(src, dst, send, recv, to):
        return pltpu.make_async_remote_copy(
            src_ref=src, dst_ref=dst, send_sem=send, recv_sem=recv, device_id=to,
            device_id_type=MESH,
        )

    load = pltpu.make_async_copy(g_ref, cols.at[z], load_sem)
    load.start()
    barrier = pltpu.get_barrier_semaphore()
    for to in (z_up, z_down, *plane, opposite, sibling):
        pl.semaphore_signal(barrier, inc=1, device_id=to, device_id_type=MESH)
    load.wait()
    pl.semaphore_wait(barrier, 8)

    def ring_copy(way, n, far):
        j = n % CHUNKS if way == 0 else CHUNKS - 1 - n % CHUNKS
        owner = (z - far + NZ) % NZ if way == 0 else (z + far) % NZ
        ref = cols.at[owner, j]
        to = z_up if way == 0 else z_down
        return remote(ref, ref, ring_send.at[way, n], ring_recv.at[way, n], to)

    def ring_start(n):
        for way in range(2):
            ring_copy(way, n, n // CHUNKS).start()

    def ring_round(n):
        for way in range(2):
            ring_copy(way, n, n // CHUNKS + 1).wait_recv()
            if n + CHUNKS < RING:
                ring_copy(way, n + CHUNKS, n // CHUNKS + 1).start()

    def ring_sent(n):
        for way in range(2):
            ring_copy(way, n, 0).wait_send()

    for n in range(CHUNKS):
        ring_start(n)

    place = dx * 4 + dy
    source = (dx < 2) & (dy % 2 == 0)

    def here(table):
        value = jnp.int32(table[0])
        for index, entry in enumerate(table[1:], 1):
            value = jnp.where(place == index, jnp.int32(entry), value)
        return value

    events = [here(table) for table in EVENTS]
    done = [here(table) for table in DONE]
    handled = [jnp.int32(0)] + [done[n // 4] // 128 ** (n % 4) % 128 for n in range(28)]

    def slice_of(k):
        return (l // 2 + k // 2) % 2 * 2 + (l + k) % 2

    def row_piece(k, q):
        part = q % 4
        part = jnp.where(slice_of(k) > l, 3 - part, part)
        return rows.at[slice_of(k), q // 4 * 4 + part]

    def set_out(k, part):
        @pl.when(source)
        def _():
            q = 4 * (2 * dx + dy // 2) + part
            chunk = jnp.where(slice_of(k) > l, 3 - part, part)
            pltpu.make_async_copy(
                cols.at[h * 4 + slice_of(k), chunk], row_piece(k, q), xy_recv.at[k, q]).start()

    def decoded(e):
        third = e // 3
        word = events[0]
        for index in range(1, len(events)):
            word = jnp.where(third == index, events[index], word)
        digit = jnp.right_shift(word, (e - third * 3) * 10)
        return digit // 16 % 4, digit % 16, [digit // (64 * 2**d) % 2 == 1 for d in range(4)]

    def onward(k, q, d):
        ref = row_piece(k, q)
        return remote(ref, ref, xy_send.at[k, 4 * q + d], xy_recv.at[k, q], plane[d])

    def take(e, carry):
        k, q, goes = decoded(e)
        onward(k, q, 0).wait_recv()
        for d in range(4):
            pl.when(goes[d])(onward(k, q, d).start)
        return carry

    def take_until(n):
        lax.fori_loop(handled[n], handled[n + 1], take, 0)

    def xy_sent(start, stop):
        def body(e, carry):
            k, q, goes = decoded(e)
            for d in range(4):
                pl.when(goes[d])(onward(k, q, d).wait_send)
            return carry

        lax.fori_loop(start, stop, body, 0)

    def squares(block):
        wide = block.astype(jnp.float32)
        wide = wide * wide
        total = wide[:, :128]
        for part in range(1, WIDTH // 128):
            total = total + wide[:, part * 128:part * 128 + 128]
        return total

    def cube(b):
        return (h + b + b // 2 - b // 3 * 2) % 4

    def multiply(b, k):
        ll = slice_of(k)
        block = cols[cube(b) * 4 + ll].reshape(ROWS, WIDTH)
        product = lax.dot_general(
            rows[ll].reshape(4 * ROWS, WIDTH), block, (((1,), (1,)), ((), ())),
            preferred_element_type=jnp.float32,
        )
        acc[b] += product.reshape(4, ROWS, 128)
        colsq[b] += squares(block)

    def row_squares(k):
        ll = slice_of(k)

        def body(i, carry):
            total = squares(rows[ll, pl.ds(4 * i, 4)].reshape(ROWS, WIDTH))
            if k:
                total = total + rowsq[i]
            rowsq[i] = total
            return carry

        lax.fori_loop(0, 4, body, 0)

    eye = lax.broadcasted_iota(jnp.int32, (128, 128), 0) == lax.broadcasted_iota(
        jnp.int32, (128, 128), 1)

    def to_lanes(folded):
        column = jnp.sum(folded, axis=1, keepdims=True)
        return jnp.sum(jnp.where(eye, column, 0.0), axis=0, keepdims=True)

    def to_rows(lanes):
        return jnp.sum(jnp.where(eye, lanes, 0.0), axis=1, keepdims=True)

    last = jnp.where(l == 0, 1, jnp.where(l == 3, 2, 3))

    for part in range(4):
        set_out(0, part)
    acc[...] = jnp.zeros_like(acc)
    colsq[...] = jnp.zeros_like(colsq)
    far = jnp.where(l < 2, 1, 2)
    near = 3 - far
    products = {
        12: [(0, 0)], 16: [(1, 0)], 17: [(2, 0)], 18: [(0, 1)], 20: [(1, 1)], 21: [(2, 1)], 22: [(0, 2)],
        23: [(near, 2)], 24: [(far, 2)], 25: [(3, 2)],
        26: [((last + 1) % 4, 3), ((last + 2) % 4, 3), ((last + 3) % 4, 3)],
    }
    row_sums = {13: 0, 19: 1, 24: 2, 26: 3}
    for tick in range(28):
        if 0 < tick <= 3 * CHUNKS:
            set_out(1 + (tick - 1) // CHUNKS, (tick - 1) % CHUNKS)
        take_until(tick)
        if tick in row_sums:
            row_squares(row_sums[tick])
        for b, k in products.get(tick, ()):
            multiply(b, k)
        ring_round(tick)
        if tick >= 8:
            ring_sent(tick - 8)
        if tick >= 16:
            xy_sent(handled[tick - 8] if tick > 16 else 0, handled[tick - 7])

    def settle():
        xy_sent(handled[20], 64)
        for n in range(20, RING):
            ring_sent(n)

    other = 1 - c
    multiply(3, 1)
    multiply(last, 3)
    for b in range(3):
        sq_out[0, b:b + 1] = to_lanes(colsq[b])
    for p in range(4):
        sq_out[0, 4 + p:5 + p] = to_lanes(rowsq[p])
    swaps = [
        remote(sq_out.at[0], sq_in.at[0], tail_send.at[0], tail_recv.at[0], sibling),
        remote(
            acc.at[pl.ds(0, 3), pl.ds(2 * other, 2)], swap_in.at[pl.ds(0, 3)], tail_send.at[1],
            tail_recv.at[1], sibling),
        remote(sq_out.at[1], sq_in.at[1], tail_send.at[2], tail_recv.at[2], sibling),
        remote(
            acc.at[3, pl.ds(2 * other, 2)], swap_in.at[3], tail_send.at[3], tail_recv.at[3],
            sibling),
    ]
    swaps[0].start()
    swaps[1].start()

    for n in range(28, RING):
        ring_round(n)

    multiply(3, 0)
    sq_out[1] = jnp.broadcast_to(to_lanes(colsq[3]), (8, 128))
    swaps[2].start()
    swaps[3].start()
    swaps[0].wait()
    scales = lax.rsqrt(sq_out[0] + sq_in[0] + 1e-6)
    swaps[1].wait()
    row_scale = [
        to_rows(jnp.where(c == 0, scales[4 + yy:5 + yy], scales[6 + yy:7 + yy]))
        for yy in range(2)
    ]
    row_here = jnp.where(big_y == 0, row_scale[0], row_scale[1])
    row_there = jnp.where(big_y == 0, row_scale[1], row_scale[0])

    def result(b, yy, row_side, col_side):
        raw = acc[b, 2 * c + yy] + swap_in[b, yy]
        value = raw * row_side * (col_side * math.sqrt(8192.0))
        return jnp.where((row_side > 0.0) & (col_side > 0.0), value, 0.0)

    for b in range(3):
        half_out[b] = result(b, 1 - big_y, row_there, scales[b:b + 1]).astype(jnp.bfloat16)
    across = [
        remote(
            half_out.at[pl.ds(0, 3)], half_in.at[pl.ds(0, 3)], tail_send.at[4],
            tail_recv.at[4], opposite),
        remote(half_out.at[3], half_in.at[3], tail_send.at[5], tail_recv.at[5], opposite),
    ]
    across[0].start()
    swaps[2].wait()
    scale = lax.rsqrt(sq_out[1] + sq_in[1] + 1e-6)[:1]
    swaps[3].wait()
    half_out[3] = result(3, 1 - big_y, row_there, scale).astype(jnp.bfloat16)
    across[1].start()

    def store(b, yy, value):
        at = pl.multiple_of((2 * cube(b) + yy) * 128, 128)
        out_ref[0, :, pl.ds(at, 128)] = value

    for b in range(4):
        value = result(b, big_y, row_here, scales[b:b + 1] if b < 3 else scale)
        if b == 0:
            value = jnp.where(eye & (2 * l + c == ex % 8), 0.0, value)
        store(b, big_y, value)
    settle()
    across[0].wait()
    for b in range(3):
        store(b, 1 - big_y, half_in[b].astype(jnp.float32))
    across[1].wait()
    store(3, 1 - big_y, half_in[3].astype(jnp.float32))
def local(grads):
    dma = pltpu.SemaphoreType.DMA
    out = pl.pallas_call(
        kernel,
        out_shape=jax.ShapeDtypeStruct((1, 128, 1024), jnp.float32),
        in_specs=[pl.BlockSpec(memory_space=pl.ANY)],
        out_specs=pl.BlockSpec(memory_space=pltpu.VMEM),
        scratch_shapes=[
            pltpu.VMEM((NZ, CHUNKS, PIECE, WIDTH), jnp.bfloat16),
            pltpu.VMEM((4, 16, PIECE, WIDTH), jnp.bfloat16),
            pltpu.VMEM((4, 4, 128, 128), jnp.float32),
            pltpu.VMEM((4, 128, 128), jnp.float32),
            pltpu.VMEM((4, 128, 128), jnp.float32),
            pltpu.VMEM((2, 8, 128), jnp.float32),
            pltpu.VMEM((2, 8, 128), jnp.float32),
            pltpu.VMEM((4, 2, 128, 128), jnp.float32),
            pltpu.VMEM((4, 128, 128), jnp.bfloat16),
            pltpu.VMEM((4, 128, 128), jnp.bfloat16),
            dma,
            dma((2, RING)),
            dma((2, RING)),
            dma((4, 64)),
            dma((4, 16)),
            dma((6,)),
            dma((6,)),
        ],
        compiler_params=pltpu.CompilerParams(
            collective_id=0, has_side_effects=True, vmem_limit_bytes=32 * 1024 * 1024
        ),
        cost_estimate=pl.CostEstimate(
            flops=2 * 512 * 512 * 4096, bytes_accessed=1 << 20, transcendentals=0),
    )(pltpu.with_memory_space_constraint(grads.reshape(CHUNKS, PIECE, WIDTH), pltpu.HBM))
    return out


def solution(mesh):
    return jax.shard_map(
        local,
        mesh=mesh,
        in_specs=(P("ex", "feat"),),
        out_specs=P("ex", "feat", None),
        check_vma=False,
    )
```
